32 devices in a mesh: row: 16 (over z, y, core), blk: 2 (over x).
Axes of the slice: x: 2, y: 2, z: 4, core: 2. Of those that a mesh axis runs over, the one named last changes fastest.
Arguments:
- field: bfloat16 [2, 256, 1024, 1024], P(None, 'blk', 'row'), may hold values from -400 to 400
- gain: float32 [256], P('blk'), may hold values from 0.1 to 1.9
- w_first: bfloat16 [2, 8, 32, 32], replicated, may hold values from -1 to 1
- b_first: float32 [2, 256], replicated, may hold values from -4 to 4
- w_second: bfloat16 [2, 8, 32, 32], replicated, may hold values from -1 to 1
- b_second: float32 [2, 256], replicated, may hold values from -4 to 4
Outputs:
- mixed: bfloat16 [2, 256, 1024, 1024], P(None, 'blk', 'row')
The draws below stay inside these ranges and needn't reach their ends.
All inputs are finite; a program needn't handle non-finite values.
Results may differ from the reference program's by a relative error of at most 0.02.
Values may be sent and summed in bfloat16 or wider, within the bound.
A program may use at most 192 MiB of HBM per device.

```python
import math
import jax
import jax.numpy as jnp
from jax import lax

SLICES = 2
CHANNELS = 256
BLOCKS = 8
BLOCK_CH = 32
HEIGHT = 1024
COLUMNS = 1024
MODES_Y = 512
MODES_X = 128


def draw_field(key, part):
    key = jax.random.fold_in(key, 7)
    key_noise, key_chan, key_pixel = jax.random.split(key, 3)
    shape_all = (SLICES, CHANNELS, HEIGHT, COLUMNS)
    chan_pos = jnp.arange(CHANNELS, dtype=jnp.float32) / CHANNELS
    noise = jnp.clip(jax.random.normal(key_noise, shape_all, jnp.float32), -6.0, 6.0)
    chan_scale = jnp.power(10.0, 0.6 * chan_pos + 0.4 * jax.random.uniform(key_chan, (CHANNELS,), jnp.float32))
    pixel_scale = jnp.power(10.0, 0.5 * jax.random.uniform(key_pixel, (SLICES, 1, HEIGHT, COLUMNS), jnp.float32))
    result = noise * chan_scale[:, None, None] * pixel_scale
    return result.astype(jnp.bfloat16)


def scatter_about(stream_key, shape, spread, limit, held_as=jnp.bfloat16):
    values = spread * jax.random.normal(stream_key, shape, jnp.float32)
    return jnp.clip(values, min=-limit, max=limit).astype(held_as)


def setup_inputs(seed: int = 0) -> dict:
    streams_of = jax.random.split(jax.random.key(seed), 7)
    field = draw_field(jax.random.fold_in(streams_of[6], 71), 0)
    gain = jnp.clip(1.0 + 0.18 * jax.random.normal(streams_of[1], (CHANNELS,), jnp.float32), 0.1, 1.9)
    w_first = scatter_about(streams_of[2], (2, BLOCKS, BLOCK_CH, BLOCK_CH), BLOCK_CH ** -0.5, 1.0)
    b_first = scatter_about(streams_of[3], (2, CHANNELS), 0.3, 4.0, jnp.float32)
    w_second = scatter_about(streams_of[4], (2, BLOCKS, BLOCK_CH, BLOCK_CH), BLOCK_CH ** -0.5, 1.0)
    b_second = scatter_about(streams_of[5], (2, CHANNELS), 0.3, 4.0, jnp.float32)
    return {"field": field, "gain": gain, "w_first": w_first, "b_first": b_first, "w_second": w_second, "b_second": b_second}


EPS = 1e-05
SHRINK = 0.01

def forward_table(count):
    positions = jnp.arange(count, dtype=jnp.int32)[:, None]
    freqs = jnp.arange(MODES_X, dtype=jnp.int32)[None, :]
    radians = (positions * freqs % count).astype(jnp.float32) * (2.0 * math.pi / count)
    norm_scale = 1.0 / math.sqrt(count)
    return jnp.stack([jnp.cos(radians) * norm_scale, -jnp.sin(radians) * norm_scale], axis=1).astype(jnp.bfloat16)

def inverse_table(count):
    freqs = jnp.arange(MODES_X, dtype=jnp.int32)[:, None]
    positions = jnp.arange(count, dtype=jnp.int32)[None, :]
    radians = (positions * freqs % count).astype(jnp.float32) * (2.0 * math.pi / count)
    weight_k = jnp.where(freqs == 0, 1.0, 2.0).astype(jnp.float32) / math.sqrt(count)
    return jnp.stack([jnp.cos(radians) * weight_k, -jnp.sin(radians) * weight_k], axis=0).astype(jnp.bfloat16)

def height_matrix(positions):
    mode_index = jnp.arange(MODES_Y, dtype=jnp.int32) - MODES_Y // 2
    phase_int = mode_index[:, None] * positions[None, :] % HEIGHT
    radians = phase_int.astype(jnp.float32) * (2.0 * math.pi / HEIGHT)
    norm_scale = 1.0 / math.sqrt(HEIGHT)
    cosine = (jnp.cos(radians) * norm_scale).astype(jnp.bfloat16)
    sine_part = (jnp.sin(radians) * norm_scale).astype(jnp.bfloat16)
    upper_rows = jnp.concatenate([cosine, sine_part], axis=1)
    lower_rows = jnp.concatenate([-sine_part, cosine], axis=1)
    return jnp.concatenate([upper_rows, lower_rows], axis=0)

def block_filter(real_spec, imag_spec, first_w, first_b, second_w, second_b):

    def mix_channels(values_in, weights):
        return jnp.einsum('mbjik,jio->mbjok', values_in, weights, precision=lax.Precision.HIGHEST)

    def widen_bias(vector):
        return vector[None, None, :, :, None]
    real_hidden = jax.nn.relu(mix_channels(real_spec, first_w[0]) - mix_channels(imag_spec, first_w[1]) + widen_bias(first_b[0]))
    imag_hidden = jax.nn.relu(mix_channels(imag_spec, first_w[0]) + mix_channels(real_spec, first_w[1]) + widen_bias(first_b[1]))
    real_out = mix_channels(real_hidden, second_w[0]) - mix_channels(imag_hidden, second_w[1]) + widen_bias(second_b[0])
    imag_out = mix_channels(imag_hidden, second_w[0]) + mix_channels(real_hidden, second_w[1]) + widen_bias(second_b[1])
    stacked = jnp.stack([real_out, imag_out])
    return (stacked - jnp.clip(stacked, -SHRINK, SHRINK)).astype(jnp.bfloat16)

def reference(field, gain, w_first, b_first, w_second, b_second):
    widened = field.astype(jnp.float32)
    average = lax.optimization_barrier(jnp.mean(widened, axis=1, keepdims=True))
    centered = widened - average
    variance = lax.optimization_barrier(jnp.mean(centered * centered, axis=1, keepdims=True))
    normed = (centered * lax.rsqrt(variance + EPS) * gain[None, :, None, None]).astype(jnp.bfloat16)
    forward = forward_table(COLUMNS).astype(jnp.float32)
    inverse = inverse_table(COLUMNS).astype(jnp.float32)
    matrix = height_matrix(jnp.arange(HEIGHT, dtype=jnp.int32))
    mat_fwd = matrix.astype(jnp.float32).reshape(2, MODES_Y, 2, HEIGHT)
    mat_inv = matrix.T.astype(jnp.float32).reshape(2, HEIGHT, 2, MODES_Y)
    grouped = jnp.moveaxis(normed.reshape(SLICES, BLOCKS, BLOCK_CH, HEIGHT, COLUMNS), 1, 0)
    first_w = jnp.moveaxis(w_first, 1, 0).astype(jnp.float32)
    second_w = jnp.moveaxis(w_second, 1, 0).astype(jnp.float32)
    first_b = jnp.moveaxis(b_first.reshape(2, BLOCKS, BLOCK_CH), 1, 0)
    second_b = jnp.moveaxis(b_second.reshape(2, BLOCKS, BLOCK_CH), 1, 0)
    highest = lax.Precision.HIGHEST

    def one_block(inputs):
        block_field, weight_one, bias_one, weight_two, bias_two = inputs
        rowspec = jnp.einsum('bchw,wrk->rbchk', block_field.astype(jnp.float32), forward, precision=highest).astype(jnp.bfloat16)
        spectrum = jnp.einsum('smrh,rbchk->smbck', mat_fwd, rowspec.astype(jnp.float32), precision=highest)
        shaped = spectrum.reshape(2, MODES_Y, SLICES, 1, BLOCK_CH, MODES_X)
        filtered = block_filter(shaped[0], shaped[1], weight_one[:, None], bias_one[:, None], weight_two[:, None], bias_two[:, None])
        filtered = filtered.reshape(2, MODES_Y, SLICES, BLOCK_CH, MODES_X)
        colfield = jnp.einsum('rhsm,smbck->rbchk', mat_inv, filtered.astype(jnp.float32), precision=highest).astype(jnp.bfloat16)
        return jnp.einsum('rbchk,rkw->bchw', colfield.astype(jnp.float32), inverse, precision=highest).astype(jnp.bfloat16)
    outputs = lax.map(one_block, (grouped, first_w, first_b, second_w, second_b))
    return jnp.moveaxis(outputs, 0, 1).reshape(SLICES, CHANNELS, HEIGHT, COLUMNS)
```

```python
import math

import jax
import jax.numpy as jnp
import numpy as np
from jax import lax
from jax.experimental import pallas as pl
from jax.experimental.pallas import tpu as pltpu
from jax.sharding import PartitionSpec as P

CHANNELS = 256
BLOCKS = 8
HEIGHT = 1024
MODES_Y = 512
MODES_X = 128


EPS = 1e-05
SHRINK = 0.01


def forward_table(count):
    positions = jnp.arange(count, dtype=jnp.int32)[:, None]
    frequency = jnp.arange(MODES_X, dtype=jnp.int32)[None, :]
    radians = (positions * frequency % count).astype(jnp.float32) * (2.0 * math.pi / count)
    norm_scale = 1.0 / math.sqrt(count)
    return jnp.stack(
        [jnp.cos(radians) * norm_scale, -jnp.sin(radians) * norm_scale], axis=1
    ).astype(jnp.bfloat16)


def inverse_table(count, frequency):
    column_freq = frequency[:, None]
    positions = jnp.arange(count, dtype=jnp.int32)[None, :]
    radians = (positions * column_freq % count).astype(jnp.float32) * (2.0 * math.pi / count)
    weight_k = jnp.where(column_freq == 0, 1.0, 2.0).astype(jnp.float32) / math.sqrt(count)
    return jnp.stack([jnp.cos(radians) * weight_k, -jnp.sin(radians) * weight_k], axis=0).astype(
        jnp.bfloat16
    )


def height_matrix(positions):
    mode_index = jnp.arange(MODES_Y, dtype=jnp.int32) - MODES_Y // 2
    phase_int = mode_index[:, None] * positions[None, :] % HEIGHT
    radians = phase_int.astype(jnp.float32) * (2.0 * math.pi / HEIGHT)
    norm_scale = 1.0 / math.sqrt(HEIGHT)
    cosine = (jnp.cos(radians) * norm_scale).astype(jnp.bfloat16)
    sine_part = (jnp.sin(radians) * norm_scale).astype(jnp.bfloat16)
    upper_rows = jnp.concatenate([cosine, sine_part], axis=1)
    lower_rows = jnp.concatenate([-sine_part, cosine], axis=1)
    return jnp.concatenate([upper_rows, lower_rows], axis=0)


def block_filter(real_spec, imag_spec, first_w, first_b, second_w, second_b):

    def mix_channels(values_in, weights):
        return jnp.einsum("mbjik,jio->mbjok", values_in, weights, precision=lax.Precision.HIGHEST)

    def widen_bias(vector):
        return vector[None, None, :, :, None]

    real_hidden = jax.nn.relu(
        mix_channels(real_spec, first_w[0])
        - mix_channels(imag_spec, first_w[1])
        + widen_bias(first_b[0])
    )
    imag_hidden = jax.nn.relu(
        mix_channels(imag_spec, first_w[0])
        + mix_channels(real_spec, first_w[1])
        + widen_bias(first_b[1])
    )
    real_out = (
        mix_channels(real_hidden, second_w[0])
        - mix_channels(imag_hidden, second_w[1])
        + widen_bias(second_b[0])
    )
    imag_out = (
        mix_channels(imag_hidden, second_w[0])
        + mix_channels(real_hidden, second_w[1])
        + widen_bias(second_b[1])
    )
    stacked = jnp.stack([real_out, imag_out])
    return (stacked - jnp.clip(stacked, -SHRINK, SHRINK)).astype(jnp.bfloat16)


def local(field, gain, w_first, b_first, w_second, b_second):
    slices, channels, rows_here, img_cols = field.shape
    channel_total = float(CHANNELS)
    widened = field.astype(jnp.float32)
    average = (
        lax.psum(jnp.sum(widened, axis=1).astype(jnp.bfloat16), "blk").astype(jnp.float32)
        / channel_total
    )
    centered = widened - average[:, None]
    variance = (
        lax.psum(jnp.sum(centered * centered, axis=1).astype(jnp.bfloat16), "blk").astype(
            jnp.float32
        )
        / channel_total
    )
    normed = (
        (widened - average[:, None])
        * lax.rsqrt(variance[:, None] + EPS)
        * gain[None, :, None, None]
    ).astype(jnp.bfloat16)
    forward = forward_table(img_cols)
    rowspec = jnp.einsum(
        "bchw,wrk->rhbck", normed, forward, preferred_element_type=jnp.float32
    ).astype(jnp.bfloat16)
    block_width = w_first.shape[2]
    group_count = lax.axis_size("blk")
    columns = lax.all_to_all(rowspec, "row", split_axis=4, concat_axis=1, tiled=True)
    blocks_here = BLOCKS // group_count
    first_block = lax.axis_index("blk") * blocks_here
    weight_one = lax.dynamic_slice_in_dim(w_first, first_block, blocks_here, 1)
    weight_two = lax.dynamic_slice_in_dim(w_second, first_block, blocks_here, 1)
    bias_one = lax.dynamic_slice_in_dim(
        b_first, first_block * block_width, blocks_here * block_width, 1
    )
    bias_two = lax.dynamic_slice_in_dim(
        b_second, first_block * block_width, blocks_here * block_width, 1
    )
    owned_channels = columns.shape[3]
    kx_here = columns.shape[4]
    block_count = weight_one.shape[1]
    matrix = height_matrix(jnp.arange(HEIGHT, dtype=jnp.int32))
    spectrum = jnp.dot(matrix, columns.reshape(2 * HEIGHT, -1), preferred_element_type=jnp.float32)
    spectrum = spectrum.reshape(2, MODES_Y, slices, block_count, block_width, kx_here)
    filtered = block_filter(
        spectrum[0],
        spectrum[1],
        weight_one.astype(jnp.float32),
        bias_one.reshape(2, block_count, block_width),
        weight_two.astype(jnp.float32),
        bias_two.reshape(2, block_count, block_width),
    )
    filtered = filtered.reshape(2, MODES_Y, slices, owned_channels, kx_here)
    product = jnp.dot(
        matrix.T, filtered.reshape(2 * MODES_Y, -1), preferred_element_type=jnp.float32
    )
    full_height = product.astype(jnp.bfloat16).reshape(2, HEIGHT, slices, owned_channels, kx_here)
    colfield = lax.all_to_all(full_height, "row", split_axis=1, concat_axis=4, tiled=True)
    frequency = jnp.arange(MODES_X, dtype=jnp.int32)
    inverse = inverse_table(img_cols, frequency)
    return jnp.einsum(
        "rhbck,rkw->bchw", colfield, inverse, preferred_element_type=jnp.float32
    ).astype(jnp.bfloat16)


LANES = 128
HALF = LANES // 2
VMEM_BYTES = 56 * 1024 * 1024


def column_tables(count, parts):
    k = np.arange(MODES_X)
    phase = (np.arange(count)[:, None] * k[None, :] % count) * (2.0 * math.pi / count)
    scale = 1.0 / math.sqrt(count)
    forward = np.stack([np.cos(phase), -np.sin(phase)], axis=1) * scale
    inverse = forward * np.where(k == 0, 1.0, 2.0)

    def order(table):
        split = table.reshape(count, 2, parts, MODES_X // parts)
        return split.transpose(0, 2, 1, 3).reshape(count, 2 * MODES_X)

    return (
        order(forward).astype(np.float32).astype(jnp.bfloat16),
        order(inverse).T.astype(np.float32).astype(jnp.bfloat16),
    )


def row_table():
    m = np.arange(MODES_Y) - MODES_Y // 2
    phase = (m[:, None] * np.arange(HEIGHT)[None, :] % HEIGHT) * (2.0 * math.pi / HEIGHT)
    table = np.concatenate([np.cos(phase), np.sin(phase)], axis=0) / math.sqrt(HEIGHT)
    return table.astype(np.float32).astype(jnp.bfloat16)


def lane_index(shape):
    return lax.broadcasted_iota(jnp.int32, shape, len(shape) - 1)


def turn(values, shift):
    return pltpu.roll(values, shift, 1)


def exchange_halves(first, second):
    low = lane_index(first.shape) < HALF
    return (
        jnp.where(low, first, turn(second, HALF)),
        jnp.where(low, turn(first, HALF), second),
    )


def swap_parts(values):
    quarter = HALF // 2
    is_real = lane_index(values.shape) % HALF < quarter
    return jnp.where(is_real, turn(values, LANES - quarter), turn(values, quarter)), is_real


def stats_kernel(field_ref, out_ref):
    channels, rows, cols = field_ref.shape[1:]
    zero = jnp.zeros((rows, cols), jnp.float32)

    def add(c, total):
        return total + field_ref[0, c].astype(jnp.float32)

    mean = lax.fori_loop(0, channels, add, zero, unroll=8) * (1.0 / channels)

    def add_square(c, total):
        centered = field_ref[0, c].astype(jnp.float32) - mean
        return total + centered * centered

    out_ref[0] = mean
    out_ref[1] = lax.fori_loop(0, channels, add_square, zero, unroll=8)


def forward_kernel(field_ref, mine_ref, other_ref, gain_ref, table_ref, out_ref, average, inv_std, normed):
    width, rows, cols = field_ref.shape[1:]
    half_width = width // 2
    group = 4
    first = pl.program_id(0) * width
    gap = mine_ref[0] - other_ref[0]
    average[...] = (mine_ref[0] + other_ref[0]) * 0.5
    variance = (mine_ref[1] + other_ref[1]) * (1.0 / CHANNELS) + gap * gap * 0.25
    inv_std[...] = lax.rsqrt(variance + EPS)
    step = 16

    @pl.loop(0, half_width // group)
    def _(g):
        for side in range(2):
            for i in range(group):
                c = side * half_width + g * group + i
                scale = gain_ref[first + c]
                for r in range(0, rows, step):
                    part = slice(r, r + step)
                    x = field_ref[0, c, part, :].astype(jnp.float32)
                    value = (x - average[part, :]) * inv_std[part, :] * scale
                    at = (side * group + i) * rows + r
                    normed[at : at + step, :] = value.astype(jnp.bfloat16)
        y = jnp.dot(normed[...], table_ref[...], preferred_element_type=jnp.float32)
        low, high = y[: group * rows], y[group * rows :]
        for p in range(2):
            lanes = slice(p * LANES, (p + 1) * LANES)
            even, odd = exchange_halves(low[:, lanes], high[:, lanes])
            for q, packed in ((2 * p, even), (2 * p + 1, odd)):
                out_ref[0, q, pl.ds(g * group, group)] = packed.astype(jnp.bfloat16).reshape(
                    group, rows, LANES
                )


def spectral_kernel(
    x_ref, fwd_ref, inv_ref, w1_ref, b1_ref, w2_ref, b2_ref, out_ref, spec, repeat
):
    owners, pairs, rows, _ = x_ref.shape
    width = 2 * pairs
    half_m = MODES_Y // 2
    tile = repeat * width

    def strided(c):
        return spec.at[pl.ds(c, half_m, stride=width), :]

    @pl.loop(0, pairs // 2)
    def _(j):
        x = jnp.concatenate(
            [x_ref[:, 2 * j + i].reshape(owners * rows, LANES) for i in range(2)], axis=1
        )
        y = jnp.dot(fwd_ref[...], x, preferred_element_type=jnp.float32)
        for i in range(2):
            lanes = slice(i * LANES, (i + 1) * LANES)
            swapped, is_real = swap_parts(y[MODES_Y:, lanes])
            s = y[:MODES_Y, lanes] + jnp.where(is_real, swapped, -swapped)
            low, high = exchange_halves(s[:half_m], s[half_m:])
            strided(2 * j + i)[...] = low
            strided(2 * j + i + pairs)[...] = high

    def mix(values, weights_ref, bias_ref):
        both = jnp.concatenate([v.astype(jnp.bfloat16) for v in values], axis=1)
        u = jnp.dot(weights_ref[0], both, preferred_element_type=jnp.float32)
        v = jnp.dot(weights_ref[1], both, preferred_element_type=jnp.float32)
        results = []
        for i in range(2):
            lanes = slice(i * LANES, (i + 1) * LANES)
            swapped, is_real = swap_parts(v[:, lanes])
            results.append(u[:, lanes] + jnp.where(is_real, -swapped, swapped) + bias_ref[...])
        return results

    @pl.loop(0, half_m * width // (2 * tile))
    def _(t):
        spots = [pl.ds(pl.multiple_of((2 * t + i) * tile, tile), tile) for i in range(2)]
        hidden = mix([spec[at, :] for at in spots], w1_ref, b1_ref)
        hidden = [jnp.maximum(h, 0.0) for h in hidden]
        for at, out in zip(spots, mix(hidden, w2_ref, b2_ref)):
            spec[at, :] = out - jnp.clip(out, -SHRINK, SHRINK)

    @pl.loop(0, pairs // 2)
    def _(j):
        columns = []
        for i in range(2):
            c = 2 * j + i
            f = jnp.concatenate(
                exchange_halves(strided(c)[...], strided(c + pairs)[...]), axis=0
            )
            swapped, is_real = swap_parts(f)
            g = jnp.where(is_real, -swapped, swapped)
            columns.append(jnp.concatenate([f, g], axis=0).astype(jnp.bfloat16))
        y = jnp.dot(
            inv_ref[...], jnp.concatenate(columns, axis=1), preferred_element_type=jnp.float32
        ).astype(jnp.bfloat16)
        for i in range(2):
            out_ref[:, 2 * j + i] = y[:, i * LANES : (i + 1) * LANES].reshape(owners, rows, LANES)


def inverse_kernel(y_ref, table_ref, *refs):
    out_ref = refs[-1]
    pairs, rows = y_ref.shape[2:4]
    group = 4

    @pl.loop(0, pairs // group)
    def _(g):
        sides = ([], [])
        for p in range(2):
            parts = [
                y_ref[0, 2 * p + i, pl.ds(g * group, group)]
                .reshape(group * rows, LANES)
                .astype(jnp.float32)
                for i in range(2)
            ]
            for side, values in zip(sides, exchange_halves(*parts)):
                side.append(values.astype(jnp.bfloat16))
        for s, side in enumerate(sides):
            mixed = jnp.dot(
                jnp.concatenate(side, axis=1), table_ref[...], preferred_element_type=jnp.float32
            )
            out_ref[0, pl.ds(s * pairs + g * group, group)] = mixed.astype(jnp.bfloat16).reshape(
                group, rows, mixed.shape[1]
            )


def params(count):
    return pltpu.CompilerParams(
        dimension_semantics=("arbitrary",) * count, vmem_limit_bytes=VMEM_BYTES
    )


def cost(flops, moved):
    return pl.CostEstimate(flops=flops, bytes_accessed=moved, transcendentals=0)


def local_stats(field, index):
    _, channels, rows, cols = field.shape
    step = 16
    return pl.pallas_call(
        stats_kernel,
        grid=(rows // step,),
        in_specs=[pl.BlockSpec((1, channels, step, cols), lambda i: (index, 0, i, 0))],
        out_specs=pl.BlockSpec((2, step, cols), lambda i: (0, i, 0)),
        out_shape=jax.ShapeDtypeStruct((2, rows, cols), jnp.float32),
        compiler_params=params(1),
        cost_estimate=cost(5 * channels * rows * cols, 2 * channels * rows * cols),
        name="stats",
    )(field)


def forward_part(field, index, mine, other, gain, table, width):
    _, channels, rows, cols = field.shape
    blocks = channels // width
    whole = lambda *shape: pl.BlockSpec(shape, lambda i: (0,) * len(shape))
    return pl.pallas_call(
        forward_kernel,
        grid=(blocks,),
        in_specs=[
            pl.BlockSpec((1, width, rows, cols), lambda i: (index, i, 0, 0)),
            whole(2, rows, cols),
            whole(2, rows, cols),
            pl.BlockSpec(memory_space=pltpu.SMEM),
            whole(*table.shape),
        ],
        out_specs=pl.BlockSpec((1, 4, width // 2, rows, LANES), lambda i: (i, 0, 0, 0, 0)),
        out_shape=jax.ShapeDtypeStruct((blocks, 4, width // 2, rows, LANES), jnp.bfloat16),
        scratch_shapes=[
            pltpu.VMEM((rows, cols), jnp.float32),
            pltpu.VMEM((rows, cols), jnp.float32),
            pltpu.VMEM((8 * rows, cols), jnp.bfloat16),
        ],
        compiler_params=params(1),
        cost_estimate=cost(4 * MODES_X * channels * rows * cols, 3 * channels * rows * cols),
        name="forward",
    )(field, mine, other, gain, table)


def spectral_part(columns, fwd, inv, weights_one, bias_one, weights_two, bias_two, repeat):
    _, pairs, _, _ = columns.shape
    vmem = pl.BlockSpec(memory_space=pltpu.VMEM)
    return pl.pallas_call(
        lambda *refs: spectral_kernel(*refs, repeat),
        in_specs=[vmem] * 7,
        out_specs=vmem,
        out_shape=jax.ShapeDtypeStruct(columns.shape, columns.dtype),
        scratch_shapes=[pltpu.VMEM((MODES_Y * pairs, LANES), jnp.float32)],
        compiler_params=pltpu.CompilerParams(vmem_limit_bytes=VMEM_BYTES),
        cost_estimate=cost(3 * 2 * HEIGHT * 2 * MODES_Y * pairs * LANES, 4 * columns.size),
        name="spectral",
    )(columns, fwd, inv, weights_one, bias_one, weights_two, bias_two)


def inverse_part(received, index, table, shape, so_far):
    blocks, parts, pairs, rows, _ = received.shape
    slices, channels, _, cols = shape
    width = 2 * pairs
    operands, specs, aliases = [received, table], [
        pl.BlockSpec((1, parts, pairs, rows, LANES), lambda i: (i, 0, 0, 0, 0)),
        pl.BlockSpec(table.shape, lambda i: (0, 0)),
    ], {}
    if so_far is not None:
        operands.append(so_far)
        specs.append(pl.BlockSpec(memory_space=pl.ANY))
        aliases = {2: 0}
    return pl.pallas_call(
        inverse_kernel,
        grid=(blocks,),
        in_specs=specs,
        out_specs=pl.BlockSpec((1, width, rows, cols), lambda i: (index, i, 0, 0)),
        out_shape=jax.ShapeDtypeStruct(shape, jnp.bfloat16),
        input_output_aliases=aliases,
        compiler_params=params(1),
        cost_estimate=cost(4 * MODES_X * channels * rows * cols, 3 * channels * rows * cols),
        name="inverse",
    )(*operands)


def local_packed(field, gain, w_first, b_first, w_second, b_second):
    slices, channels, rows, cols = field.shape
    width = w_first.shape[2]
    blocks_here = channels // width
    fwd_cols, inv_cols = (jnp.asarray(t) for t in column_tables(cols, 4))
    table = row_table()
    fwd_rows, inv_rows = jnp.asarray(table), jnp.asarray(np.ascontiguousarray(table.T))

    block = lax.axis_index("blk") * blocks_here + lax.axis_index("row") // 4
    repeat = 256 // width

    def spread(weights):
        here = lax.dynamic_index_in_dim(weights, block, 1, keepdims=False)
        eye = jnp.eye(repeat, dtype=here.dtype)
        tiled = eye[None, :, None, :, None] * jnp.swapaxes(here, 1, 2)[:, None, :, None, :]
        return tiled.reshape(2, repeat * width, repeat * width)

    def widen(bias):
        here = lax.dynamic_slice_in_dim(bias, block * width, width, 1)
        is_real = np.arange(LANES) % HALF < HALF // 2
        tile = jnp.where(is_real[None, :], here[0][:, None], here[1][:, None])
        return jnp.tile(tile, (repeat, 1))

    layers = (spread(w_first), widen(b_first), spread(w_second), widen(b_second))
    swap = [(0, 1), (1, 0)]
    packed, others = [], []
    for b in range(slices):
        mine = local_stats(field, b)
        others.append((mine, lax.ppermute(mine, "blk", swap)))
    for b, (mine, other) in enumerate(others):
        part = forward_part(field, b, mine, other, gain, fwd_cols, width)
        packed.append(part.reshape((-1,) + part.shape[2:]))

    def send(values):
        return lax.all_to_all(values, "row", split_axis=0, concat_axis=0, tiled=True)

    received = []
    columns = send(packed[0])
    for b in range(slices):
        following = None
        if b + 1 < slices:
            columns, ready = lax.optimization_barrier((columns, packed[b + 1]))
            following = send(ready)
        filtered = spectral_part(columns, fwd_rows, inv_rows, *layers, repeat)
        if received:
            received[-1], filtered = lax.optimization_barrier((received[-1], filtered))
        received.append(send(filtered))
        columns = following
    mixed = None
    for b, back in enumerate(received):
        back = back.reshape((blocks_here, 4) + back.shape[1:])
        mixed = inverse_part(back, b, inv_cols, field.shape, mixed)
    return mixed


def packs(mesh, channels, width):
    groups, owners = mesh.shape["blk"], mesh.shape["row"]
    return groups == 2 and owners == 4 * (channels // groups // width) and HEIGHT % (16 * owners) == 0


def solution(mesh):
    def whole(field, gain, w_first, b_first, w_second, b_second):
        packed = packs(mesh, field.shape[1], w_first.shape[2])
        return jax.shard_map(
            local_packed if packed else local,
            mesh=mesh,
            in_specs=(P(None, "blk", "row", None), P("blk"), P(), P(), P(), P()),
            out_specs=P(None, "blk", "row", None),
            check_vma=False,
        )(field, gain, w_first, b_first, w_second, b_second)

    return whole
```

```python
import math

import jax
import jax.numpy as jnp
import numpy as np
from jax import lax
from jax.experimental import pallas as pl
from jax.experimental.pallas import tpu as pltpu
from jax.sharding import PartitionSpec as P

CHANNELS = 256
BLOCKS = 8
HEIGHT = 1024
MODES_Y = 512
MODES_X = 128


EPS = 1e-05
SHRINK = 0.01


def forward_table(count):
    positions = jnp.arange(count, dtype=jnp.int32)[:, None]
    frequency = jnp.arange(MODES_X, dtype=jnp.int32)[None, :]
    radians = (positions * frequency % count).astype(jnp.float32) * (2.0 * math.pi / count)
    norm_scale = 1.0 / math.sqrt(count)
    return jnp.stack(
        [jnp.cos(radians) * norm_scale, -jnp.sin(radians) * norm_scale], axis=1
    ).astype(jnp.bfloat16)


def inverse_table(count, frequency):
    column_freq = frequency[:, None]
    positions = jnp.arange(count, dtype=jnp.int32)[None, :]
    radians = (positions * column_freq % count).astype(jnp.float32) * (2.0 * math.pi / count)
    weight_k = jnp.where(column_freq == 0, 1.0, 2.0).astype(jnp.float32) / math.sqrt(count)
    return jnp.stack([jnp.cos(radians) * weight_k, -jnp.sin(radians) * weight_k], axis=0).astype(
        jnp.bfloat16
    )


def height_matrix(positions):
    mode_index = jnp.arange(MODES_Y, dtype=jnp.int32) - MODES_Y // 2
    phase_int = mode_index[:, None] * positions[None, :] % HEIGHT
    radians = phase_int.astype(jnp.float32) * (2.0 * math.pi / HEIGHT)
    norm_scale = 1.0 / math.sqrt(HEIGHT)
    cosine = (jnp.cos(radians) * norm_scale).astype(jnp.bfloat16)
    sine_part = (jnp.sin(radians) * norm_scale).astype(jnp.bfloat16)
    upper_rows = jnp.concatenate([cosine, sine_part], axis=1)
    lower_rows = jnp.concatenate([-sine_part, cosine], axis=1)
    return jnp.concatenate([upper_rows, lower_rows], axis=0)


def block_filter(real_spec, imag_spec, first_w, first_b, second_w, second_b):

    def mix_channels(values_in, weights):
        return jnp.einsum("mbjik,jio->mbjok", values_in, weights, precision=lax.Precision.HIGHEST)

    def widen_bias(vector):
        return vector[None, None, :, :, None]

    real_hidden = jax.nn.relu(
        mix_channels(real_spec, first_w[0])
        - mix_channels(imag_spec, first_w[1])
        + widen_bias(first_b[0])
    )
    imag_hidden = jax.nn.relu(
        mix_channels(imag_spec, first_w[0])
        + mix_channels(real_spec, first_w[1])
        + widen_bias(first_b[1])
    )
    real_out = (
        mix_channels(real_hidden, second_w[0])
        - mix_channels(imag_hidden, second_w[1])
        + widen_bias(second_b[0])
    )
    imag_out = (
        mix_channels(imag_hidden, second_w[0])
        + mix_channels(real_hidden, second_w[1])
        + widen_bias(second_b[1])
    )
    stacked = jnp.stack([real_out, imag_out])
    return (stacked - jnp.clip(stacked, -SHRINK, SHRINK)).astype(jnp.bfloat16)


def local(field, gain, w_first, b_first, w_second, b_second):
    slices, channels, rows_here, img_cols = field.shape
    channel_total = float(CHANNELS)
    widened = field.astype(jnp.float32)
    average = (
        lax.psum(jnp.sum(widened, axis=1).astype(jnp.bfloat16), "blk").astype(jnp.float32)
        / channel_total
    )
    centered = widened - average[:, None]
    variance = (
        lax.psum(jnp.sum(centered * centered, axis=1).astype(jnp.bfloat16), "blk").astype(
            jnp.float32
        )
        / channel_total
    )
    normed = (
        (widened - average[:, None])
        * lax.rsqrt(variance[:, None] + EPS)
        * gain[None, :, None, None]
    ).astype(jnp.bfloat16)
    forward = forward_table(img_cols)
    rowspec = jnp.einsum(
        "bchw,wrk->rhbck", normed, forward, preferred_element_type=jnp.float32
    ).astype(jnp.bfloat16)
    block_width = w_first.shape[2]
    group_count = lax.axis_size("blk")
    columns = lax.all_to_all(rowspec, "row", split_axis=4, concat_axis=1, tiled=True)
    blocks_here = BLOCKS // group_count
    first_block = lax.axis_index("blk") * blocks_here
    weight_one = lax.dynamic_slice_in_dim(w_first, first_block, blocks_here, 1)
    weight_two = lax.dynamic_slice_in_dim(w_second, first_block, blocks_here, 1)
    bias_one = lax.dynamic_slice_in_dim(
        b_first, first_block * block_width, blocks_here * block_width, 1
    )
    bias_two = lax.dynamic_slice_in_dim(
        b_second, first_block * block_width, blocks_here * block_width, 1
    )
    owned_channels = columns.shape[3]
    kx_here = columns.shape[4]
    block_count = weight_one.shape[1]
    matrix = height_matrix(jnp.arange(HEIGHT, dtype=jnp.int32))
    spectrum = jnp.dot(matrix, columns.reshape(2 * HEIGHT, -1), preferred_element_type=jnp.float32)
    spectrum = spectrum.reshape(2, MODES_Y, slices, block_count, block_width, kx_here)
    filtered = block_filter(
        spectrum[0],
        spectrum[1],
        weight_one.astype(jnp.float32),
        bias_one.reshape(2, block_count, block_width),
        weight_two.astype(jnp.float32),
        bias_two.reshape(2, block_count, block_width),
    )
    filtered = filtered.reshape(2, MODES_Y, slices, owned_channels, kx_here)
    product = jnp.dot(
        matrix.T, filtered.reshape(2 * MODES_Y, -1), preferred_element_type=jnp.float32
    )
    full_height = product.astype(jnp.bfloat16).reshape(2, HEIGHT, slices, owned_channels, kx_here)
    colfield = lax.all_to_all(full_height, "row", split_axis=1, concat_axis=4, tiled=True)
    frequency = jnp.arange(MODES_X, dtype=jnp.int32)
    inverse = inverse_table(img_cols, frequency)
    return jnp.einsum(
        "rhbck,rkw->bchw", colfield, inverse, preferred_element_type=jnp.float32
    ).astype(jnp.bfloat16)


LANES = 128
HALF = LANES // 2
TILE_ROWS = 256
VMEM_BYTES = 56 * 1024 * 1024


def column_tables(count, parts):
    k = np.arange(MODES_X)
    phase = (np.arange(count)[:, None] * k[None, :] % count) * (2.0 * math.pi / count)
    scale = 1.0 / math.sqrt(count)
    forward = np.stack([np.cos(phase), -np.sin(phase)], axis=1) * scale
    inverse = forward * np.where(k == 0, 1.0, 2.0)

    def order(table):
        split = table.reshape(count, 2, parts, MODES_X // parts)
        return split.transpose(0, 2, 1, 3).reshape(count, 2 * MODES_X)

    return (
        order(forward).astype(np.float32).astype(jnp.bfloat16),
        order(inverse).T.astype(np.float32).astype(jnp.bfloat16),
    )


def row_table():
    m = np.arange(MODES_Y) - MODES_Y // 2
    phase = (m[:, None] * np.arange(HEIGHT)[None, :] % HEIGHT) * (2.0 * math.pi / HEIGHT)
    table = np.concatenate([np.cos(phase), np.sin(phase)], axis=0) / math.sqrt(HEIGHT)
    return table.astype(np.float32).astype(jnp.bfloat16)


def lane_index(shape):
    return lax.broadcasted_iota(jnp.int32, shape, len(shape) - 1)


def turn(values, shift):
    return pltpu.roll(values, shift, 1)


def exchange_halves(first, second):
    low = lane_index(first.shape) < HALF
    return (
        jnp.where(low, first, turn(second, HALF)),
        jnp.where(low, turn(first, HALF), second),
    )


def swap_parts(values):
    quarter = HALF // 2
    is_real = lane_index(values.shape) % HALF < quarter
    return jnp.where(is_real, turn(values, LANES - quarter), turn(values, quarter)), is_real


def stats_kernel(field_ref, *refs):
    out_ref = refs[-1]
    channels, rows, cols = field_ref.shape[1:]
    span = cols // 2
    for start in range(0, cols, span):
        lanes = slice(start, start + span)
        pivot = field_ref[0, 0, :, lanes].astype(jnp.float32)
        zero = jnp.zeros((rows, span), jnp.float32)

        def add(c, totals):
            moved = field_ref[0, c, :, lanes].astype(jnp.float32) - pivot
            return totals[0] + moved, totals[1] + moved * moved

        total, squares = lax.fori_loop(0, channels, add, (zero, zero), unroll=8)
        offset = total * (1.0 / channels)
        out_ref[0, :, lanes] = pivot + offset
        out_ref[1, :, lanes] = jnp.maximum(squares - total * offset, 0.0)


def forward_kernel(field_ref, mine_ref, other_ref, gain_ref, table_ref, *refs):
    out_ref, average, inv_std, normed = refs[-4:]
    width, rows, cols = field_ref.shape[1:]
    half_width = width // 2
    group = min(half_width, TILE_ROWS // rows)
    groups = half_width // group
    first = pl.program_id(0) * width
    gap = mine_ref[0] - other_ref[0]
    average[...] = (mine_ref[0] + other_ref[0]) * 0.5
    variance = (mine_ref[1] + other_ref[1]) * (1.0 / CHANNELS) + gap * gap * 0.25
    inv_std[...] = lax.rsqrt(variance + EPS)
    step = 16

    def normalize(g):
        for side in range(2):
            for i in range(group):
                c = side * half_width + g * group + i
                scale = gain_ref[first + c]
                for r in range(0, rows, step):
                    part = slice(r, r + step)
                    x = field_ref[0, c, part, :].astype(jnp.float32)
                    value = (x - average[part, :]) * inv_std[part, :] * scale
                    at = (side * group + i) * rows + r
                    normed[g, at : at + step, :] = value.astype(jnp.bfloat16)

    normalize(0)
    for g in range(groups):
        if g + 1 < groups:
            normalize(g + 1)
        y = jnp.dot(normed[g], table_ref[...], preferred_element_type=jnp.float32)
        low, high = y[: group * rows], y[group * rows :]
        for p in range(2):
            lanes = slice(p * LANES, (p + 1) * LANES)
            even, odd = exchange_halves(low[:, lanes], high[:, lanes])
            for q, packed in ((2 * p, even), (2 * p + 1, odd)):
                out_ref[0, q, g * group : (g + 1) * group] = packed.astype(jnp.bfloat16).reshape(
                    group, rows, LANES
                )


def spectral_kernel(
    x_ref, fwd_ref, inv_ref, w1_ref, b1_ref, w2_ref, b2_ref, out_ref, spec, repeat
):
    owners, pairs, rows, _ = x_ref.shape
    width = 2 * pairs
    half_m = MODES_Y // 2
    tile = repeat * width

    def strided(c):
        return spec.at[pl.ds(c, half_m, stride=width), :]

    @pl.loop(0, pairs // 2)
    def _(j):
        x = jnp.concatenate(
            [x_ref[:, 2 * j + i].reshape(owners * rows, LANES) for i in range(2)], axis=1
        )
        y = jnp.dot(fwd_ref[...], x, preferred_element_type=jnp.float32)
        for i in range(2):
            lanes = slice(i * LANES, (i + 1) * LANES)
            swapped, is_real = swap_parts(y[MODES_Y:, lanes])
            s = y[:MODES_Y, lanes] + jnp.where(is_real, swapped, -swapped)
            low, high = exchange_halves(s[:half_m], s[half_m:])
            strided(2 * j + i)[...] = low
            strided(2 * j + i + pairs)[...] = high

    def mix(values, weights_ref, bias_ref):
        both = jnp.concatenate([v.astype(jnp.bfloat16) for v in values], axis=1)
        u = jnp.dot(weights_ref[0], both, preferred_element_type=jnp.float32)
        v = jnp.dot(weights_ref[1], both, preferred_element_type=jnp.float32)
        results = []
        for i in range(2):
            lanes = slice(i * LANES, (i + 1) * LANES)
            swapped, is_real = swap_parts(v[:, lanes])
            results.append(u[:, lanes] + jnp.where(is_real, -swapped, swapped) + bias_ref[...])
        return results

    @pl.loop(0, half_m * width // (2 * tile))
    def _(t):
        spots = [pl.ds(pl.multiple_of((2 * t + i) * tile, tile), tile) for i in range(2)]
        hidden = mix([spec[at, :] for at in spots], w1_ref, b1_ref)
        hidden = [jnp.maximum(h, 0.0) for h in hidden]
        for at, out in zip(spots, mix(hidden, w2_ref, b2_ref)):
            spec[at, :] = out - jnp.clip(out, -SHRINK, SHRINK)

    @pl.loop(0, pairs // 2)
    def _(j):
        columns = []
        for i in range(2):
            c = 2 * j + i
            f = jnp.concatenate(
                exchange_halves(strided(c)[...], strided(c + pairs)[...]), axis=0
            )
            swapped, is_real = swap_parts(f)
            g = jnp.where(is_real, -swapped, swapped)
            columns.append(jnp.concatenate([f, g], axis=0).astype(jnp.bfloat16))
        y = jnp.dot(
            inv_ref[...], jnp.concatenate(columns, axis=1), preferred_element_type=jnp.float32
        ).astype(jnp.bfloat16)
        for i in range(2):
            out_ref[:, 2 * j + i] = y[:, i * LANES : (i + 1) * LANES].reshape(owners, rows, LANES)


def inverse_kernel(y_ref, table_ref, *refs):
    out_ref = refs[-1]
    pairs, rows = y_ref.shape[2:4]
    group = min(pairs, TILE_ROWS // rows)
    for at in range(0, pairs, group):
        sides = ([], [])
        for p in range(2):
            parts = [
                y_ref[0, 2 * p + i, at : at + group]
                .reshape(group * rows, LANES)
                .astype(jnp.float32)
                for i in range(2)
            ]
            for side, values in zip(sides, exchange_halves(*parts)):
                side.append(values.astype(jnp.bfloat16))
        for s, side in enumerate(sides):
            mixed = jnp.dot(
                jnp.concatenate(side, axis=1), table_ref[...], preferred_element_type=jnp.float32
            )
            out_ref[0, s * pairs + at : s * pairs + at + group] = mixed.astype(
                jnp.bfloat16
            ).reshape(group, rows, mixed.shape[1])


def params(count):
    return pltpu.CompilerParams(
        dimension_semantics=("arbitrary",) * count, vmem_limit_bytes=VMEM_BYTES
    )


def cost(flops, moved):
    return pl.CostEstimate(flops=flops, bytes_accessed=moved, transcendentals=0)


def local_stats(field, index, part, parts, after):
    _, channels, rows, cols = field.shape
    step = 16
    rows //= parts
    steps = rows // step
    return pl.pallas_call(
        stats_kernel,
        grid=(steps,),
        in_specs=[
            pl.BlockSpec((1, channels, step, cols), lambda i: (index, 0, part * steps + i, 0))
        ]
        + [pl.BlockSpec(memory_space=pl.ANY)] * len(after),
        out_specs=pl.BlockSpec((2, step, cols), lambda i: (0, i, 0)),
        out_shape=jax.ShapeDtypeStruct((2, rows, cols), jnp.float32),
        compiler_params=params(1),
        cost_estimate=cost(5 * channels * rows * cols, 2 * channels * rows * cols),
        name="stats",
    )(field, *after)


def forward_part(field, index, part, parts, stats, gain, table, width, so_far):
    _, channels, all_rows, cols = field.shape
    rows = all_rows // parts
    blocks = channels // width
    half_width = width // 2
    group = min(half_width, TILE_ROWS // rows)
    whole = lambda *shape: pl.BlockSpec(shape, lambda i: (0,) * len(shape))
    operands = [field, *stats, gain, table]
    specs = [
        pl.BlockSpec((1, width, rows, cols), lambda i: (index, i, part, 0)),
        whole(2, rows, cols),
        whole(2, rows, cols),
        pl.BlockSpec(memory_space=pltpu.SMEM),
        whole(*table.shape),
    ]
    aliases = {}
    if so_far is not None:
        aliases = {len(operands): 0}
        operands.append(so_far)
        specs.append(pl.BlockSpec(memory_space=pl.ANY))
    return pl.pallas_call(
        forward_kernel,
        grid=(blocks,),
        in_specs=specs,
        out_specs=pl.BlockSpec((1, 4, half_width, rows, LANES), lambda i: (i, 0, 0, part, 0)),
        out_shape=jax.ShapeDtypeStruct((blocks, 4, half_width, all_rows, LANES), jnp.bfloat16),
        input_output_aliases=aliases,
        scratch_shapes=[
            pltpu.VMEM((rows, cols), jnp.float32),
            pltpu.VMEM((rows, cols), jnp.float32),
            pltpu.VMEM((half_width // group, 2 * group * rows, cols), jnp.bfloat16),
        ],
        compiler_params=params(1),
        cost_estimate=cost(4 * MODES_X * channels * rows * cols, 3 * channels * rows * cols),
        name="forward",
    )(*operands)


def spectral_part(columns, fwd, inv, weights_one, bias_one, weights_two, bias_two, repeat):
    _, pairs, _, _ = columns.shape
    vmem = pl.BlockSpec(memory_space=pltpu.VMEM)
    return pl.pallas_call(
        lambda *refs: spectral_kernel(*refs, repeat),
        in_specs=[vmem] * 7,
        out_specs=vmem,
        out_shape=jax.ShapeDtypeStruct(columns.shape, columns.dtype),
        scratch_shapes=[pltpu.VMEM((MODES_Y * pairs, LANES), jnp.float32)],
        compiler_params=pltpu.CompilerParams(vmem_limit_bytes=VMEM_BYTES),
        cost_estimate=cost(3 * 2 * HEIGHT * 2 * MODES_Y * pairs * LANES, 4 * columns.size),
        name="spectral",
    )(columns, fwd, inv, weights_one, bias_one, weights_two, bias_two)


def inverse_part(received, index, table, shape, so_far):
    blocks, parts, pairs, rows, _ = received.shape
    slices, channels, _, cols = shape
    width = 2 * pairs
    step = rows // 2
    operands, specs, aliases = [received, table], [
        pl.BlockSpec((1, parts, pairs, step, LANES), lambda i, j: (i, 0, 0, j, 0)),
        pl.BlockSpec(table.shape, lambda i, j: (0, 0)),
    ], {}
    if so_far is not None:
        operands.append(so_far)
        specs.append(pl.BlockSpec(memory_space=pl.ANY))
        aliases = {2: 0}
    return pl.pallas_call(
        inverse_kernel,
        grid=(blocks, rows // step),
        in_specs=specs,
        out_specs=pl.BlockSpec((1, width, step, cols), lambda i, j: (index, i, j, 0)),
        out_shape=jax.ShapeDtypeStruct(shape, jnp.bfloat16),
        input_output_aliases=aliases,
        compiler_params=params(2),
        cost_estimate=cost(4 * MODES_X * channels * rows * cols, 3 * channels * rows * cols),
        name="inverse",
    )(*operands)


def local_packed(field, gain, w_first, b_first, w_second, b_second):
    slices, channels, rows, cols = field.shape
    width = w_first.shape[2]
    blocks_here = channels // width
    fwd_cols, inv_cols = (jnp.asarray(t) for t in column_tables(cols, 4))
    table = row_table()
    fwd_rows, inv_rows = jnp.asarray(table), jnp.asarray(np.ascontiguousarray(table.T))

    block = lax.axis_index("blk") * blocks_here + lax.axis_index("row") // 4
    repeat = 256 // width

    def spread(weights):
        here = lax.dynamic_index_in_dim(weights, block, 1, keepdims=False)
        eye = jnp.eye(repeat, dtype=here.dtype)
        tiled = eye[None, :, None, :, None] * jnp.swapaxes(here, 1, 2)[:, None, :, None, :]
        return tiled.reshape(2, repeat * width, repeat * width)

    def widen(bias):
        here = lax.dynamic_slice_in_dim(bias, block * width, width, 1)
        is_real = np.arange(LANES) % HALF < HALF // 2
        tile = jnp.where(is_real[None, :], here[0][:, None], here[1][:, None])
        return jnp.tile(tile, (repeat, 1))

    layers = (spread(w_first), widen(b_first), spread(w_second), widen(b_second))
    swap = [(0, 1), (1, 0)]
    parts = [2] + [1] * (slices - 1)
    packed, after = [], []
    for b in range(slices):
        stats = []
        for part in range(parts[b]):
            mine = local_stats(field, b, part, parts[b], after)
            stats.append((mine, lax.ppermute(mine, "blk", swap)))
            after = [mine]
        result = None
        for part, pair in enumerate(stats):
            result = forward_part(
                field, b, part, parts[b], pair, gain, fwd_cols, width, result
            )
        after = [result]
        packed.append(result.reshape((-1,) + result.shape[2:]))

    def send(values):
        return lax.all_to_all(values, "row", split_axis=0, concat_axis=0, tiled=True)

    received = []
    columns = send(packed[0])
    for b in range(slices):
        following = None
        if b + 1 < slices:
            columns, ready = lax.optimization_barrier((columns, packed[b + 1]))
            following = send(ready)
        filtered = spectral_part(columns, fwd_rows, inv_rows, *layers, repeat)
        if received:
            received[-1], filtered = lax.optimization_barrier((received[-1], filtered))
        received.append(send(filtered))
        columns = following
    mixed = None
    for b, back in enumerate(received):
        back = back.reshape((blocks_here, 4) + back.shape[1:])
        mixed = inverse_part(back, b, inv_cols, field.shape, mixed)
    return mixed


def packs(mesh, channels, width):
    groups, owners = mesh.shape["blk"], mesh.shape["row"]
    return groups == 2 and owners == 4 * (channels // groups // width) and HEIGHT % (32 * owners) == 0


def solution(mesh):
    def whole(field, gain, w_first, b_first, w_second, b_second):
        packed = packs(mesh, field.shape[1], w_first.shape[2])
        return jax.shard_map(
            local_packed if packed else local,
            mesh=mesh,
            in_specs=(P(None, "blk", "row", None), P("blk"), P(), P(), P(), P()),
            out_specs=P(None, "blk", "row", None),
            check_vma=False,
        )(field, gain, w_first, b_first, w_second, b_second)

    return whole
```

```python
import math

import jax
import jax.numpy as jnp
import numpy as np
from jax import lax
from jax.experimental import pallas as pl
from jax.experimental.pallas import tpu as pltpu
from jax.sharding import PartitionSpec as P

CHANNELS = 256
BLOCKS = 8
HEIGHT = 1024
MODES_Y = 512
MODES_X = 128


EPS = 1e-05
SHRINK = 0.01


def forward_table(count):
    positions = jnp.arange(count, dtype=jnp.int32)[:, None]
    frequency = jnp.arange(MODES_X, dtype=jnp.int32)[None, :]
    radians = (positions * frequency % count).astype(jnp.float32) * (2.0 * math.pi / count)
    norm_scale = 1.0 / math.sqrt(count)
    return jnp.stack(
        [jnp.cos(radians) * norm_scale, -jnp.sin(radians) * norm_scale], axis=1
    ).astype(jnp.bfloat16)


def inverse_table(count, frequency):
    column_freq = frequency[:, None]
    positions = jnp.arange(count, dtype=jnp.int32)[None, :]
    radians = (positions * column_freq % count).astype(jnp.float32) * (2.0 * math.pi / count)
    weight_k = jnp.where(column_freq == 0, 1.0, 2.0).astype(jnp.float32) / math.sqrt(count)
    return jnp.stack([jnp.cos(radians) * weight_k, -jnp.sin(radians) * weight_k], axis=0).astype(
        jnp.bfloat16
    )


def height_matrix(positions):
    mode_index = jnp.arange(MODES_Y, dtype=jnp.int32) - MODES_Y // 2
    phase_int = mode_index[:, None] * positions[None, :] % HEIGHT
    radians = phase_int.astype(jnp.float32) * (2.0 * math.pi / HEIGHT)
    norm_scale = 1.0 / math.sqrt(HEIGHT)
    cosine = (jnp.cos(radians) * norm_scale).astype(jnp.bfloat16)
    sine_part = (jnp.sin(radians) * norm_scale).astype(jnp.bfloat16)
    upper_rows = jnp.concatenate([cosine, sine_part], axis=1)
    lower_rows = jnp.concatenate([-sine_part, cosine], axis=1)
    return jnp.concatenate([upper_rows, lower_rows], axis=0)


def block_filter(real_spec, imag_spec, first_w, first_b, second_w, second_b):

    def mix_channels(values_in, weights):
        return jnp.einsum("mbjik,jio->mbjok", values_in, weights, precision=lax.Precision.HIGHEST)

    def widen_bias(vector):
        return vector[None, None, :, :, None]

    real_hidden = jax.nn.relu(
        mix_channels(real_spec, first_w[0])
        - mix_channels(imag_spec, first_w[1])
        + widen_bias(first_b[0])
    )
    imag_hidden = jax.nn.relu(
        mix_channels(imag_spec, first_w[0])
        + mix_channels(real_spec, first_w[1])
        + widen_bias(first_b[1])
    )
    real_out = (
        mix_channels(real_hidden, second_w[0])
        - mix_channels(imag_hidden, second_w[1])
        + widen_bias(second_b[0])
    )
    imag_out = (
        mix_channels(imag_hidden, second_w[0])
        + mix_channels(real_hidden, second_w[1])
        + widen_bias(second_b[1])
    )
    stacked = jnp.stack([real_out, imag_out])
    return (stacked - jnp.clip(stacked, -SHRINK, SHRINK)).astype(jnp.bfloat16)


def local(field, gain, w_first, b_first, w_second, b_second):
    slices, channels, rows_here, img_cols = field.shape
    channel_total = float(CHANNELS)
    widened = field.astype(jnp.float32)
    average = (
        lax.psum(jnp.sum(widened, axis=1).astype(jnp.bfloat16), "blk").astype(jnp.float32)
        / channel_total
    )
    centered = widened - average[:, None]
    variance = (
        lax.psum(jnp.sum(centered * centered, axis=1).astype(jnp.bfloat16), "blk").astype(
            jnp.float32
        )
        / channel_total
    )
    normed = (
        (widened - average[:, None])
        * lax.rsqrt(variance[:, None] + EPS)
        * gain[None, :, None, None]
    ).astype(jnp.bfloat16)
    forward = forward_table(img_cols)
    rowspec = jnp.einsum(
        "bchw,wrk->rhbck", normed, forward, preferred_element_type=jnp.float32
    ).astype(jnp.bfloat16)
    block_width = w_first.shape[2]
    group_count = lax.axis_size("blk")
    columns = lax.all_to_all(rowspec, "row", split_axis=4, concat_axis=1, tiled=True)
    blocks_here = BLOCKS // group_count
    first_block = lax.axis_index("blk") * blocks_here
    weight_one = lax.dynamic_slice_in_dim(w_first, first_block, blocks_here, 1)
    weight_two = lax.dynamic_slice_in_dim(w_second, first_block, blocks_here, 1)
    bias_one = lax.dynamic_slice_in_dim(
        b_first, first_block * block_width, blocks_here * block_width, 1
    )
    bias_two = lax.dynamic_slice_in_dim(
        b_second, first_block * block_width, blocks_here * block_width, 1
    )
    owned_channels = columns.shape[3]
    kx_here = columns.shape[4]
    block_count = weight_one.shape[1]
    matrix = height_matrix(jnp.arange(HEIGHT, dtype=jnp.int32))
    spectrum = jnp.dot(matrix, columns.reshape(2 * HEIGHT, -1), preferred_element_type=jnp.float32)
    spectrum = spectrum.reshape(2, MODES_Y, slices, block_count, block_width, kx_here)
    filtered = block_filter(
        spectrum[0],
        spectrum[1],
        weight_one.astype(jnp.float32),
        bias_one.reshape(2, block_count, block_width),
        weight_two.astype(jnp.float32),
        bias_two.reshape(2, block_count, block_width),
    )
    filtered = filtered.reshape(2, MODES_Y, slices, owned_channels, kx_here)
    product = jnp.dot(
        matrix.T, filtered.reshape(2 * MODES_Y, -1), preferred_element_type=jnp.float32
    )
    full_height = product.astype(jnp.bfloat16).reshape(2, HEIGHT, slices, owned_channels, kx_here)
    colfield = lax.all_to_all(full_height, "row", split_axis=1, concat_axis=4, tiled=True)
    frequency = jnp.arange(MODES_X, dtype=jnp.int32)
    inverse = inverse_table(img_cols, frequency)
    return jnp.einsum(
        "rhbck,rkw->bchw", colfield, inverse, preferred_element_type=jnp.float32
    ).astype(jnp.bfloat16)


LANES = 128
HALF = LANES // 2
TILE_ROWS = 256
VMEM_BYTES = 56 * 1024 * 1024


def column_tables(count, parts):
    k = np.arange(MODES_X)
    phase = (np.arange(count)[:, None] * k[None, :] % count) * (2.0 * math.pi / count)
    scale = 1.0 / math.sqrt(count)
    forward = np.stack([np.cos(phase), -np.sin(phase)], axis=1) * scale
    inverse = forward * np.where(k == 0, 1.0, 2.0)

    def order(table):
        split = table.reshape(count, 2, parts, MODES_X // parts)
        return split.transpose(0, 2, 1, 3).reshape(count, 2 * MODES_X)

    return (
        order(forward).astype(np.float32).astype(jnp.bfloat16),
        order(inverse).T.astype(np.float32).astype(jnp.bfloat16),
    )


def row_table():
    m = np.arange(MODES_Y) - MODES_Y // 2
    phase = (m[:, None] * np.arange(HEIGHT)[None, :] % HEIGHT) * (2.0 * math.pi / HEIGHT)
    table = np.concatenate([np.cos(phase), np.sin(phase)], axis=0) / math.sqrt(HEIGHT)
    return table.astype(np.float32).astype(jnp.bfloat16)


def lane_index(shape):
    return lax.broadcasted_iota(jnp.int32, shape, len(shape) - 1)


def turn(values, shift):
    return pltpu.roll(values, shift, 1)


def exchange_halves(first, second):
    low = lane_index(first.shape) < HALF
    return (
        jnp.where(low, first, turn(second, HALF)),
        jnp.where(low, turn(first, HALF), second),
    )


def swap_parts(values):
    quarter = HALF // 2
    is_real = lane_index(values.shape) % HALF < quarter
    return jnp.where(is_real, turn(values, LANES - quarter), turn(values, quarter)), is_real


def stats_kernel(field_ref, *refs):
    out_ref = refs[-1]
    channels, rows, cols = field_ref.shape[1:]
    span = cols // 2
    for start in range(0, cols, span):
        lanes = slice(start, start + span)
        pivot = field_ref[0, 0, :, lanes].astype(jnp.float32)
        zero = jnp.zeros((rows, span), jnp.float32)

        def add(c, totals):
            moved = field_ref[0, c, :, lanes].astype(jnp.float32) - pivot
            return totals[0] + moved, totals[1] + moved * moved

        total, squares = lax.fori_loop(0, channels, add, (zero, zero), unroll=8)
        offset = total * (1.0 / channels)
        out_ref[0, :, lanes] = pivot + offset
        out_ref[1, :, lanes] = jnp.maximum(squares - total * offset, 0.0)


def forward_kernel(field_ref, mine_ref, other_ref, gain_ref, table_ref, *refs):
    out_ref, average, inv_std, normed = refs[-4:]
    width, rows, cols = field_ref.shape[1:]
    half_width = width // 2
    group = min(half_width, TILE_ROWS // rows)
    groups = half_width // group
    first = pl.program_id(0) * width
    gap = mine_ref[0] - other_ref[0]
    average[...] = (mine_ref[0] + other_ref[0]) * 0.5
    variance = (mine_ref[1] + other_ref[1]) * (1.0 / CHANNELS) + gap * gap * 0.25
    inv_std[...] = lax.rsqrt(variance + EPS)
    step = 16

    def normalize(g):
        for side in range(2):
            for i in range(group):
                c = side * half_width + g * group + i
                scale = gain_ref[first + c]
                for r in range(0, rows, step):
                    part = slice(r, r + step)
                    x = field_ref[0, c, part, :].astype(jnp.float32)
                    value = (x - average[part, :]) * inv_std[part, :] * scale
                    at = (side * group + i) * rows + r
                    normed[g, at : at + step, :] = value.astype(jnp.bfloat16)

    normalize(0)
    for g in range(groups):
        if g + 1 < groups:
            normalize(g + 1)
        y = jnp.dot(normed[g], table_ref[...], preferred_element_type=jnp.float32)
        low, high = y[: group * rows], y[group * rows :]
        for p in range(2):
            lanes = slice(p * LANES, (p + 1) * LANES)
            even, odd = exchange_halves(low[:, lanes], high[:, lanes])
            for q, packed in ((2 * p, even), (2 * p + 1, odd)):
                out_ref[0, q, g * group : (g + 1) * group] = packed.astype(jnp.bfloat16).reshape(
                    group, rows, LANES
                )


def spectral_kernel(
    x_ref, fwd_ref, inv_ref, w1_ref, b1_ref, w2_ref, b2_ref, out_ref, spec, repeat
):
    owners, pairs, rows, _ = x_ref.shape
    width = 2 * pairs
    half_m = MODES_Y // 2
    tile = repeat * width

    def strided(c):
        return spec.at[pl.ds(c, half_m, stride=width), :]

    @pl.loop(0, pairs // 2)
    def _(j):
        x = jnp.concatenate(
            [x_ref[:, 2 * j + i].reshape(owners * rows, LANES) for i in range(2)], axis=1
        )
        y = jnp.dot(fwd_ref[...], x, preferred_element_type=jnp.float32)
        for i in range(2):
            lanes = slice(i * LANES, (i + 1) * LANES)
            swapped, is_real = swap_parts(y[MODES_Y:, lanes])
            s = y[:MODES_Y, lanes] + jnp.where(is_real, swapped, -swapped)
            low, high = exchange_halves(s[:half_m], s[half_m:])
            strided(2 * j + i)[...] = low
            strided(2 * j + i + pairs)[...] = high

    def mix(values, weights_ref, bias_ref):
        both = jnp.concatenate([v.astype(jnp.bfloat16) for v in values], axis=1)
        u = jnp.dot(weights_ref[0], both, preferred_element_type=jnp.float32)
        v = jnp.dot(weights_ref[1], both, preferred_element_type=jnp.float32)
        results = []
        for i in range(2):
            lanes = slice(i * LANES, (i + 1) * LANES)
            swapped, is_real = swap_parts(v[:, lanes])
            results.append(u[:, lanes] + jnp.where(is_real, -swapped, swapped) + bias_ref[...])
        return results

    @pl.loop(0, half_m * width // (2 * tile))
    def _(t):
        spots = [pl.ds(pl.multiple_of((2 * t + i) * tile, tile), tile) for i in range(2)]
        hidden = mix([spec[at, :] for at in spots], w1_ref, b1_ref)
        hidden = [jnp.maximum(h, 0.0) for h in hidden]
        for at, out in zip(spots, mix(hidden, w2_ref, b2_ref)):
            spec[at, :] = out - jnp.clip(out, -SHRINK, SHRINK)

    @pl.loop(0, pairs // 2)
    def _(j):
        columns = []
        for i in range(2):
            c = 2 * j + i
            f = jnp.concatenate(
                exchange_halves(strided(c)[...], strided(c + pairs)[...]), axis=0
            )
            swapped, is_real = swap_parts(f)
            g = jnp.where(is_real, -swapped, swapped)
            columns.append(jnp.concatenate([f, g], axis=0).astype(jnp.bfloat16))
        y = jnp.dot(
            inv_ref[...], jnp.concatenate(columns, axis=1), preferred_element_type=jnp.float32
        ).astype(jnp.bfloat16)
        for i in range(2):
            out_ref[:, 2 * j + i] = y[:, i * LANES : (i + 1) * LANES].reshape(owners, rows, LANES)


def inverse_kernel(y_ref, table_ref, *refs):
    out_ref = refs[-1]
    pairs, rows = y_ref.shape[2:4]
    group = min(pairs, TILE_ROWS // rows)
    for at in range(0, pairs, group):
        sides = ([], [])
        for p in range(2):
            parts = [
                y_ref[0, 2 * p + i, at : at + group]
                .reshape(group * rows, LANES)
                .astype(jnp.float32)
                for i in range(2)
            ]
            for side, values in zip(sides, exchange_halves(*parts)):
                side.append(values.astype(jnp.bfloat16))
        for s, side in enumerate(sides):
            mixed = jnp.dot(
                jnp.concatenate(side, axis=1), table_ref[...], preferred_element_type=jnp.float32
            )
            out_ref[0, s * pairs + at : s * pairs + at + group] = mixed.astype(
                jnp.bfloat16
            ).reshape(group, rows, mixed.shape[1])


def params(count):
    return pltpu.CompilerParams(
        dimension_semantics=("arbitrary",) * count, vmem_limit_bytes=VMEM_BYTES
    )


def cost(flops, moved):
    return pl.CostEstimate(flops=flops, bytes_accessed=moved, transcendentals=0)


def local_stats(field, index, part, parts, after):
    _, channels, rows, cols = field.shape
    step = 16
    rows //= parts
    steps = rows // step
    return pl.pallas_call(
        stats_kernel,
        grid=(steps,),
        in_specs=[
            pl.BlockSpec((1, channels, step, cols), lambda i: (index, 0, part * steps + i, 0))
        ]
        + [pl.BlockSpec(memory_space=pl.ANY)] * len(after),
        out_specs=pl.BlockSpec((2, step, cols), lambda i: (0, i, 0)),
        out_shape=jax.ShapeDtypeStruct((2, rows, cols), jnp.float32),
        compiler_params=params(1),
        cost_estimate=cost(5 * channels * rows * cols, 2 * channels * rows * cols),
        name="stats",
    )(field, *after)


def forward_part(field, index, part, parts, stats, gain, table, width, so_far):
    _, channels, all_rows, cols = field.shape
    rows = all_rows // parts
    blocks = channels // width
    half_width = width // 2
    group = min(half_width, TILE_ROWS // rows)
    whole = lambda *shape: pl.BlockSpec(shape, lambda i: (0,) * len(shape))
    operands = [field, *stats, gain, table]
    specs = [
        pl.BlockSpec((1, width, rows, cols), lambda i: (index, i, part, 0)),
        whole(2, rows, cols),
        whole(2, rows, cols),
        pl.BlockSpec(memory_space=pltpu.SMEM),
        whole(*table.shape),
    ]
    aliases = {}
    if so_far is not None:
        aliases = {len(operands): 0}
        operands.append(so_far)
        specs.append(pl.BlockSpec(memory_space=pl.ANY))
    return pl.pallas_call(
        forward_kernel,
        grid=(blocks,),
        in_specs=specs,
        out_specs=pl.BlockSpec((1, 4, half_width, rows, LANES), lambda i: (i, 0, 0, part, 0)),
        out_shape=jax.ShapeDtypeStruct((blocks, 4, half_width, all_rows, LANES), jnp.bfloat16),
        input_output_aliases=aliases,
        scratch_shapes=[
            pltpu.VMEM((rows, cols), jnp.float32),
            pltpu.VMEM((rows, cols), jnp.float32),
            pltpu.VMEM((half_width // group, 2 * group * rows, cols), jnp.bfloat16),
        ],
        compiler_params=params(1),
        cost_estimate=cost(4 * MODES_X * channels * rows * cols, 3 * channels * rows * cols),
        name="forward",
    )(*operands)


def spectral_part(columns, fwd, inv, weights_one, bias_one, weights_two, bias_two, repeat):
    _, pairs, _, _ = columns.shape
    vmem = pl.BlockSpec(memory_space=pltpu.VMEM)
    return pl.pallas_call(
        lambda *refs: spectral_kernel(*refs, repeat),
        in_specs=[vmem] * 7,
        out_specs=vmem,
        out_shape=jax.ShapeDtypeStruct(columns.shape, columns.dtype),
        scratch_shapes=[pltpu.VMEM((MODES_Y * pairs, LANES), jnp.float32)],
        compiler_params=pltpu.CompilerParams(vmem_limit_bytes=VMEM_BYTES),
        cost_estimate=cost(3 * 2 * HEIGHT * 2 * MODES_Y * pairs * LANES, 4 * columns.size),
        name="spectral",
    )(columns, fwd, inv, weights_one, bias_one, weights_two, bias_two)


def inverse_part(received, index, table, shape, so_far):
    blocks, parts, pairs, rows, _ = received.shape
    slices, channels, _, cols = shape
    width = 2 * pairs
    step = rows // 2
    operands, specs, aliases = [received, table], [
        pl.BlockSpec((1, parts, pairs, step, LANES), lambda i, j: (i, 0, 0, j, 0)),
        pl.BlockSpec(table.shape, lambda i, j: (0, 0)),
    ], {}
    if so_far is not None:
        operands.append(so_far)
        specs.append(pl.BlockSpec(memory_space=pl.ANY))
        aliases = {2: 0}
    return pl.pallas_call(
        inverse_kernel,
        grid=(blocks, rows // step),
        in_specs=specs,
        out_specs=pl.BlockSpec((1, width, step, cols), lambda i, j: (index, i, j, 0)),
        out_shape=jax.ShapeDtypeStruct(shape, jnp.bfloat16),
        input_output_aliases=aliases,
        compiler_params=params(2),
        cost_estimate=cost(4 * MODES_X * channels * rows * cols, 3 * channels * rows * cols),
        name="inverse",
    )(*operands)


def local_packed(field, gain, w_first, b_first, w_second, b_second):
    slices, channels, rows, cols = field.shape
    width = w_first.shape[2]
    blocks_here = channels // width
    fwd_cols, inv_cols = (jnp.asarray(t) for t in column_tables(cols, 4))
    table = row_table()
    fwd_rows, inv_rows = jnp.asarray(table), jnp.asarray(np.ascontiguousarray(table.T))

    block = lax.axis_index("blk") * blocks_here + lax.axis_index("row") // 4
    repeat = 256 // width

    def spread(weights):
        here = lax.dynamic_index_in_dim(weights, block, 1, keepdims=False)
        eye = jnp.eye(repeat, dtype=here.dtype)
        tiled = eye[None, :, None, :, None] * jnp.swapaxes(here, 1, 2)[:, None, :, None, :]
        return tiled.reshape(2, repeat * width, repeat * width)

    def widen(bias):
        here = lax.dynamic_slice_in_dim(bias, block * width, width, 1)
        is_real = np.arange(LANES) % HALF < HALF // 2
        tile = jnp.where(is_real[None, :], here[0][:, None], here[1][:, None])
        return jnp.tile(tile, (repeat, 1))

    layers = (spread(w_first), widen(b_first), spread(w_second), widen(b_second))
    swap = [(0, 1), (1, 0)]
    parts = [2] + [1] * (slices - 1)
    packed, after = [], []
    for b in range(slices):
        stats = []
        for part in range(parts[b]):
            mine = local_stats(field, b, part, parts[b], after)
            stats.append((mine, lax.ppermute(mine, "blk", swap)))
            after = [mine]
        result = None
        for part, pair in enumerate(stats):
            result = forward_part(
                field, b, part, parts[b], pair, gain, fwd_cols, width, result
            )
        after = [result]
        packed.append(result.reshape((-1,) + result.shape[2:]))

    def send(values):
        return lax.all_to_all(values, "row", split_axis=0, concat_axis=0, tiled=True)

    received = []
    columns = send(packed[0])
    for b in range(slices):
        following = None
        if b + 1 < slices:
            following = send(packed[b + 1])
        filtered = spectral_part(columns, fwd_rows, inv_rows, *layers, repeat)
        received.append(send(filtered))
        columns = following
    mixed = None
    for b, back in enumerate(received):
        back = back.reshape((blocks_here, 4) + back.shape[1:])
        mixed = inverse_part(back, b, inv_cols, field.shape, mixed)
    return mixed


def packs(mesh, channels, width):
    groups, owners = mesh.shape["blk"], mesh.shape["row"]
    return groups == 2 and owners == 4 * (channels // groups // width) and HEIGHT % (32 * owners) == 0


def solution(mesh):
    def whole(field, gain, w_first, b_first, w_second, b_second):
        packed = packs(mesh, field.shape[1], w_first.shape[2])
        return jax.shard_map(
            local_packed if packed else local,
            mesh=mesh,
            in_specs=(P(None, "blk", "row", None), P("blk"), P(), P(), P(), P()),
            out_specs=P(None, "blk", "row", None),
            check_vma=False,
        )(field, gain, w_first, b_first, w_second, b_second)

    return whole
```
